32 devices in a mesh: group: 2 (over core), fsdp: 4 (over y, x), ep: 4 (over z).
Axes of the slice: x: 2, y: 2, z: 4, core: 2. Of those that a mesh axis runs over, the one named last changes fastest.
Arguments:
- batch: bfloat16 [2, 4, 512, 1536], P('group', None, 'fsdp'), may hold values from -6 to 6
- expert_ids: int32 [2, 4, 512, 4], P('group', None, 'fsdp'), may hold values from 0 to 7, all different within a row; in each aligned block of 128 rows (0 to 127, 128 to 255, ..., all dimensions but the last counted through in order) at most 96 rows name the same one
- route_weights: float32 [2, 4, 512, 4], P('group', None, 'fsdp'), may hold values from 0.1 to 1
- weights: bfloat16 [4, 3, 1536, 1536], P('ep', None, 'fsdp'), may hold values from -0.15625 to 0.15625
- cotangent: bfloat16 [4, 512, 1536], P(None, 'fsdp'), may hold values from -6 to 6
- master: float32 [4, 3, 1536, 1536], P('ep', None, 'fsdp', 'group'), may hold values from -0.15625 to 0.15625
- moment_one: float32 [4, 3, 1536, 1536], P('ep', None, 'fsdp', 'group'), may hold values from -0.013258252 to 0.013258252
- moment_two: float32 [4, 3, 1536, 1536], P('ep', None, 'fsdp', 'group'), may hold values from 8.789063e-09 to 1.7578125e-07
Outputs:
- layer_out: bfloat16 [2, 4, 512, 1536], P('group', None, ('fsdp', 'ep'))
- master_next: float32 [4, 3, 1536, 1536], P('ep', None, 'fsdp', 'group')
- moment_one_next: float32 [4, 3, 1536, 1536], P('ep', None, 'fsdp', 'group')
- moment_two_next: float32 [4, 3, 1536, 1536], P('ep', None, 'fsdp', 'group')
- serving: bfloat16 [4, 3, 1536, 1536], P('ep', None, 'fsdp')
The draws below stay inside these ranges and needn't reach their ends.
Inputs may be any that keep to these rules, and one draw needn't show every extreme that they name: `expert_ids`: the 4 ids of a row differ. In each aligned block of 128 rows (one step of one fsdp index in one slot) no expert is named more than 96 times, a bound that some block reaches.
All inputs are finite; a program needn't handle non-finite values.
Results may differ from the reference program's by a relative error of at most 0.019.
Values may be sent and summed in bfloat16 or wider, within the bound.
A program may use at most 192 MiB of HBM per device.

```python
import math
import jax
import jax.numpy as jnp
import numpy as np
from jax import lax

D = 1536
F = 1536
NE = 8
TOP = 4
STEPS = 4
R = 128
E = 4
CAP = 96
NR = 512
N_FSDP = 4


def moment_base():
    return 0.3 / math.sqrt(STEPS * NR)


def draw_moment_one(key, part):
    key = jax.random.fold_in(key, 11)
    shape = (E, 3, D, F)
    values = 0.5 * jax.random.truncated_normal(key, -4.0, 4.0, shape, jnp.float32)
    return moment_base() * values


def draw_moment_two(key, part):
    key = jax.random.fold_in(key, 23)
    shape = (E, 3, D, F)
    lower = 0.0002
    upper = 0.004
    spread = jax.random.uniform(key, shape, jnp.float32, math.log(lower), math.log(upper))
    values = jnp.exp(spread)
    base = moment_base()
    return base * base * values


def levels(stream_key, shape, shards, low, high):
    def one(position, shards_of):
        steps = jax.random.uniform(jax.random.fold_in(jax.random.fold_in(stream_key, 6), position), (shards_of,), jnp.float32, low / len(shards), high / len(shards))
        return jnp.repeat(jnp.exp(steps), shape[position] // shards_of).reshape((-1,) + (1,) * (len(shape) - position - 1))

    level = one(*shards[0])
    for cut in shards[1:]:
        level = level * one(*cut)
    return level


def deal_out(rng, own, number, rows, number_of, top, bound, slope):
    sequence = jax.random.permutation(rng, number_of)
    crowded, common = shares(number_of, rows * top, bound, slope, True), shares(number_of, rows * top, bound, slope, False)
    places = jnp.arange(number_of)

    def named(lengths, turn):
        used = int((lengths > 0).sum())
        fixed = max(1, used // 4)
        shifted = fixed + (places - fixed + turn * (used - fixed)) % max(1, number_of - fixed)
        return jnp.zeros((number_of,), jnp.int32).at[sequence[jnp.where(places < fixed, places, shifted)]].set(jnp.asarray(lengths, jnp.int32))

    lengths = jnp.where(number % 4 == 0, named(crowded, number // 4), named(common, number - number // 4 - 1))
    mixed = jax.random.permutation(jax.random.fold_in(own, 3), number_of)
    giver, receiver = mixed[0:number_of // 2 * 2:2], mixed[1:number_of // 2 * 2:2]
    slack = jnp.minimum(lengths[giver] - 1, bound - lengths[receiver]) // 2
    slack = jnp.where((giver == sequence[0]) | (receiver == sequence[0]) | (lengths[receiver] == 0), 0, jnp.maximum(slack, 0))
    shifted = jax.random.randint(jax.random.fold_in(own, 4), (number_of // 2,), 0, 1 << 20) % (slack + 1)
    lengths = lengths.at[giver].add(-shifted).at[receiver].add(shifted)
    members = jnp.searchsorted(jnp.cumsum(lengths), jnp.arange(rows * top), side="right").astype(jnp.int32)
    table = members.reshape(top, rows).T
    table = table[jax.random.permutation(jax.random.fold_in(own, 1), rows)]
    turn = jax.random.randint(jax.random.fold_in(own, 2), (rows, 1), 0, top)
    return jnp.take_along_axis(table, (jnp.arange(top)[None, :] + turn) % top, axis=1)


def shares(count, total, bound, skew, full):
    loads = [(1 << 20) // math.isqrt(rank ** skew) + 1 for rank in range(1, count + 1)]
    largest = bound if full else min(bound, max(-(-total // count), total * loads[0] // sum(loads)))
    least = 1 if total - largest >= count - 1 else 0
    given, surplus = [largest] + [least] * (count - 1), total - largest - least * (count - 1)
    while surplus > 0:
        free = [i for i in range(1, count) if given[i] < largest] or [i for i in range(1, count) if given[i] < bound]
        mass, budget = sum([loads[i] for i in free]), surplus
        for i in free:
            extra = min(bound - given[i], max(1, budget * loads[i] // mass), surplus)
            given[i] = given[i] + extra
            surplus = surplus - extra
    return np.array(given)


def normal_values(key, shape, scale, most, cuts=(), held_as=jnp.bfloat16):
    values = jax.random.normal(key, shape, jnp.float32) * scale
    if len(cuts) > 0:
        values = levels(key, shape, cuts, -0.22, 0.18) * values
    return jnp.clip(values, min=-most, max=most).astype(held_as)


def setup_inputs(seed: int = 0) -> dict:
    keys = jax.random.split(jax.random.key(seed), 9)
    batch = normal_values(keys[0], (2, STEPS, NR, D), 1.0, 6.0, ((0, 2), (2, 4)))
    expert_ids_keys = jax.random.split(jax.random.fold_in(keys[1], 1), 2 * STEPS * NR // R)
    expert_ids_turns = jax.random.permutation(jax.random.fold_in(keys[1], 3), 2 * STEPS * NR // R)
    expert_ids = jax.vmap(lambda own, number: deal_out(jax.random.fold_in(keys[1], 2), own, number, R, NE, TOP, CAP, 1))(expert_ids_keys, expert_ids_turns).reshape((2, STEPS, NR, TOP))
    route_weights = jnp.clip(0.1 + 0.9 * jax.random.uniform(keys[2], (2, STEPS, NR, TOP), jnp.float32) ** levels(keys[2], (2, STEPS, NR, TOP), ((0, 2), (2, 4)), -0.2, 0.2), 0.1, 1.0)
    weights = normal_values(keys[3], (E, 3, D, F), D ** -0.5, 0.15625, ((0, 4), (2, 4)))
    cotangent = normal_values(keys[4], (STEPS, NR, D), 1.0, 6.0, ((1, 4),))
    master = normal_values(keys[5], (E, 3, D, F), D ** -0.5, 0.15625, ((0, 4), (2, 4), (3, 2)), jnp.float32)
    moment_one = draw_moment_one(jax.random.fold_in(keys[8], 71), 0)
    moment_two = draw_moment_two(jax.random.fold_in(keys[8], 71), 0)
    return dict(batch=batch, expert_ids=expert_ids, route_weights=route_weights, weights=weights, cotangent=cotangent, master=master, moment_one=moment_one, moment_two=moment_two)


GLU_ALPHA = 1.702
BETA_ONE = 0.9
BETA_TWO = 0.999
LEARN_RATE = 0.01
ADAM_EPS = 1e-08
BIAS_ONE = 1.0 - 0.9 ** 10
BIAS_TWO = 1.0 - 0.999 ** 10

def expert_coef(route_ids, route_probs, expert):
    return lax.optimization_barrier(jnp.sum(jnp.where(route_ids == expert, route_probs, jnp.float32(0.0)), axis=-1))

def expert_pass(tokens, expert_weights, coef):
    gate_pre = jnp.dot(tokens, expert_weights[0], preferred_element_type=jnp.float32)
    up_pre = jnp.dot(tokens, expert_weights[1], preferred_element_type=jnp.float32)
    sig_gate = jax.nn.sigmoid(GLU_ALPHA * gate_pre)
    activated = gate_pre * sig_gate
    hidden = (activated * (up_pre + 1.0)).astype(jnp.bfloat16)
    projected = jnp.dot(hidden, expert_weights[2].T, preferred_element_type=jnp.float32)
    term = (coef[:, None] * projected).astype(jnp.bfloat16)
    return (gate_pre, up_pre, sig_gate, activated, hidden, term)

def slot_forward(tokens, route_ids, route_probs, weights):

    def one_step(operands):
        step_tokens, step_ids, step_probs = operands
        summed = jnp.zeros(step_tokens.shape, jnp.float32)
        for expert in range(E):
            coef = expert_coef(step_ids, step_probs, expert)
            summed = summed + expert_pass(step_tokens, weights[expert], coef)[5].astype(jnp.float32)
        return summed.astype(jnp.bfloat16)
    return lax.map(one_step, (tokens, route_ids, route_probs))

def block_grads(tokens, upstream, coef, expert_weights):
    gate_pre, up_pre, sig_gate, activated, hidden, unused = expert_pass(tokens, expert_weights, coef)
    dy_scaled = (coef[:, None] * upstream.astype(jnp.float32)).astype(jnp.bfloat16)
    grad_down = jnp.dot(dy_scaled.T, hidden, preferred_element_type=jnp.float32)
    grad_hidden = jnp.dot(dy_scaled, expert_weights[2], preferred_element_type=jnp.float32)
    gate_slope = sig_gate + GLU_ALPHA * gate_pre * sig_gate * (1.0 - sig_gate)
    d_up = (grad_hidden * activated).astype(jnp.bfloat16)
    d_gate = (grad_hidden * (up_pre + 1.0) * gate_slope).astype(jnp.bfloat16)
    grad_gate = jnp.dot(tokens.T, d_gate, preferred_element_type=jnp.float32)
    grad_up = jnp.dot(tokens.T, d_up, preferred_element_type=jnp.float32)
    return jnp.stack([grad_gate, grad_up, grad_down])

def by_block(array):
    tail = array.shape[2:]
    split = array.reshape((STEPS, N_FSDP, R) + tail)
    return jnp.moveaxis(split, 1, 0).reshape((N_FSDP, STEPS * R) + tail)

def learner_grads(tokens, upstream, route_ids, route_probs, weights):
    blocks = (by_block(tokens), by_block(upstream), by_block(route_ids), by_block(route_probs))
    per_expert = []
    for expert in range(E):

        def add_block(summed, operands, expert=expert):
            block_tokens, block_up, block_ids, block_probs = operands
            coef = expert_coef(block_ids, block_probs, expert)
            part = block_grads(block_tokens, block_up, coef, weights[expert]) / (STEPS * NR)
            rounded = lax.optimization_barrier(part.astype(jnp.bfloat16))
            return (summed + rounded.astype(jnp.float32), None)
        summed, unused = lax.scan(add_block, jnp.zeros((3, D, F), jnp.float32), blocks)
        per_expert.append(summed)
    return jnp.stack(per_expert)

def reference(batch, expert_ids, route_weights, weights, cotangent, master, moment_one, moment_two):
    layer_out = jnp.stack([slot_forward(batch[slot_index], expert_ids[slot_index], route_weights[slot_index], weights) for slot_index in range(2)])
    grad = learner_grads(batch[0], cotangent, expert_ids[0], route_weights[0], weights)
    moment_one_next = BETA_ONE * moment_one + (1.0 - BETA_ONE) * grad
    moment_two_next = BETA_TWO * moment_two + (1.0 - BETA_TWO) * grad * grad
    master_next = master - LEARN_RATE * (moment_one_next / BIAS_ONE) / (jnp.sqrt(moment_two_next / BIAS_TWO) + ADAM_EPS)
    serving = master_next.astype(jnp.bfloat16)
    return (layer_out, master_next, moment_one_next, moment_two_next, serving)
```

```python
import functools

import jax
import jax.numpy as jnp
from jax import lax
from jax.experimental import pallas as pl
from jax.experimental.pallas import tpu as pltpu
from jax.sharding import PartitionSpec as P

CAP = 96
MESH = pl.DeviceIdType.MESH
GLU_ALPHA = 1.702
BETA_ONE = 0.9
BETA_TWO = 0.999
LEARN_RATE = 0.01
ADAM_EPS = 1e-08
BIAS_ONE = 1.0 - 0.9**10
BIAS_TWO = 1.0 - 0.999**10


def shifted(value, axis, steps):
    count = lax.axis_size(axis)
    leading, last = (max(0, -steps), min(count, count - steps))
    return lax.ppermute(value, axis, [(source, source + steps) for source in range(leading, last)])


def contract_rows(left, right):
    return lax.dot_general(
        left, right, (((0,), (0,)), ((), ())), preferred_element_type=jnp.float32
    )


def adam(grad_own, master, moment_one, moment_two):
    moment_one_next = BETA_ONE * moment_one + (1.0 - BETA_ONE) * grad_own
    moment_two_next = BETA_TWO * moment_two + (1.0 - BETA_TWO) * grad_own * grad_own
    master_next = master - LEARN_RATE * (moment_one_next / BIAS_ONE) / (
        jnp.sqrt(moment_two_next / BIAS_TWO) + ADAM_EPS
    )
    return master_next, moment_one_next, moment_two_next


def layer_kernel(
    ep_count, tokens_total, ids, probs, x, ct, w, lo_out, grad_out,
    wts, gate, up, gh, onehots, coefs, xs, dys, gx, gdy, hid, gb, gs, sg,
    r1x, r1y, px, py, rt, rr,
    own_sem, dsx, drx, dsy, dry, fsx, frx, fsy, fry, psend, precv,
    lsend, lrecv, r1s, r1r, pps, ppr, es, er,
):
    g, f, e = lax.axis_index("group"), lax.axis_index("fsdp"), lax.axis_index("ep")
    fx, fy = f % 2, f // 2
    xn, yn, dn, pg = fy * 2 + 1 - fx, (1 - fy) * 2 + fx, 3 - f, 1 - g
    steps, row_count, feat = x.shape
    dep = w.shape[1]
    half_rows, quarter = dep // 2, dep // 4
    hidden_count = w.shape[2]
    half_cols = hidden_count // 2
    slots = steps * CAP
    x_id, y_id, p_id = (g, xn, e), (g, yn, e), (pg, f, e)
    order = (2, 0, 1)

    barrier = pltpu.get_barrier_semaphore()
    peers = [(g, f, (e + k) % ep_count) for k in range(1, ep_count)]
    greet = [x_id, y_id, p_id] + peers
    for peer in greet:
        pl.semaphore_signal(barrier, inc=1, device_id=peer, device_id_type=MESH)
    pl.semaphore_wait(barrier, len(greet))

    def remote(src, dst, send, recv, target):
        return pltpu.make_async_remote_copy(
            src_ref=src, dst_ref=dst, send_sem=send, recv_sem=recv,
            device_id=target, device_id_type=MESH,
        )

    base = pl.multiple_of(g * half_rows, half_rows)
    mine = pl.ds(base, half_rows)
    first = pl.ds(base, quarter)
    second = pl.ds(pl.multiple_of(base + quarter, quarter), quarter)

    def direct(m):
        return (
            remote(w.at[m, mine], wts.at[m, f, mine], dsx.at[m], drx.at[m], x_id),
            remote(w.at[m, mine], wts.at[m, f, mine], dsy.at[m], dry.at[m], y_id),
        )

    def relays(m):
        return (
            remote(wts.at[m, xn, first], wts.at[m, xn, first], fsy.at[m], fry.at[m], y_id),
            remote(wts.at[m, yn, second], wts.at[m, yn, second], fsx.at[m], frx.at[m], x_id),
        )

    def share(m, place, source):
        block = wts.at[m, source, mine]
        return remote(block, block, psend.at[m, place], precv.at[m, place], p_id)

    directs = {m: direct(m) for m in order}
    forwards = {m: relays(m) for m in order}
    shares = {m: [share(m, i, s) for i, s in enumerate((xn, yn, dn))] for m in order}

    for m in order[:2]:
        for copy in directs[m]:
            copy.start()
    owns = [pltpu.make_async_copy(w.at[m], wts.at[m, f], own_sem.at[m]) for m in range(3)]
    for copy in owns:
        copy.start()

    match = ids[...] == e
    row_coef = jnp.sum(jnp.where(match, probs[...], 0.0), axis=0)
    routed = jnp.max(jnp.where(match, 1.0, 0.0), axis=0)
    before = (
        lax.broadcasted_iota(jnp.int32, (row_count, row_count), 0)
        < lax.broadcasted_iota(jnp.int32, (row_count, row_count), 1)
    )
    rank = jnp.dot(
        routed.astype(jnp.bfloat16),
        jnp.where(before, 1.0, 0.0).astype(jnp.bfloat16),
        preferred_element_type=jnp.float32,
    ).astype(jnp.int32)
    slot_iota = lax.broadcasted_iota(jnp.int32, (CAP, row_count), 0)
    for s in range(steps):
        hit = jnp.where(slot_iota == rank[s : s + 1, :], routed[s : s + 1, :], 0.0)
        onehots[s] = hit.astype(jnp.bfloat16)
        coef = jnp.sum(hit * row_coef[s : s + 1, :], axis=1, keepdims=True)
        coefs[pl.ds(s * CAP, CAP), :] = jnp.broadcast_to(coef, (CAP, 128))

    @pl.loop(0, steps)
    def _(s):
        place = pl.ds(pl.multiple_of(s * CAP, CAP), CAP)
        picker = onehots[s]
        coef = coefs[place, :][:, 0:1]
        for c in range(4):
            cols = pl.ds(c * dep, dep)
            picked = jnp.dot(picker, x[s, :, cols], preferred_element_type=jnp.float32)
            xs[c, place, :] = picked.astype(jnp.bfloat16)
            picked = jnp.dot(picker, ct[s, :, cols], preferred_element_type=jnp.float32)
            dys[c, place, :] = (coef * picked).astype(jnp.bfloat16)

    to_rollout = [
        remote(xs, gx, lsend.at[0], lrecv.at[0], p_id),
        remote(dys, gdy, lsend.at[1], lrecv.at[1], p_id),
    ] + [
        remote(gs.at[i], gb.at[i], lsend.at[2 + i], lrecv.at[2 + i], p_id) for i in range(3)
    ]

    @pl.when(g == 0)
    def _():
        to_rollout[0].start()
        to_rollout[1].start()
        gx[...] = xs[...]
        gdy[...] = dys[...]

    tile = 512

    def accumulate(m, source, start=False):
        total, left = ((gate, xs), (up, xs), (gh, dys))[m]

        @pl.loop(0, hidden_count // tile)
        def _(n):
            cols = pl.ds(pl.multiple_of(n * tile, tile), tile)
            part = jnp.dot(left[source], wts[m, source, :, cols], preferred_element_type=jnp.float32)
            total[:, cols] = part if start else total[:, cols] + part

    for m in order:
        owns[m].wait()
        accumulate(m, f, True)

    def take_direct(m, later):
        to_x, to_y = directs[m]
        relay_y, relay_x = forwards[m]
        to_x.wait_recv()
        relay_y.start()
        shares[m][0].start()
        to_y.wait_recv()
        relay_x.start()
        shares[m][1].start()
        if later is not None:
            for copy in directs[later]:
                copy.start()
        shares[m][0].wait_recv()
        accumulate(m, xn)
        shares[m][1].wait_recv()
        accumulate(m, yn)

    def take_diagonal(m):
        relay_y, relay_x = forwards[m]
        relay_y.wait_recv()
        relay_x.wait_recv()
        shares[m][2].start()
        shares[m][2].wait_recv()
        accumulate(m, dn)

    take_direct(order[0], order[2])
    take_direct(order[1], None)
    take_diagonal(order[0])
    take_direct(order[2], None)
    take_diagonal(order[1])
    take_diagonal(order[2])

    block = 16

    @pl.loop(0, slots // block)
    def _(b):
        rows = pl.ds(pl.multiple_of(b * block, block), block)
        for side in range(2):
            cols = pl.ds(side * half_cols, half_cols)
            gate_pre, up_one = gate[rows, cols], up[rows, cols] + 1.0
            back = gh[rows, cols]
            sig = 1.0 / (1.0 + jnp.exp(-GLU_ALPHA * gate_pre))
            act = gate_pre * sig
            value = (act * up_one).astype(jnp.bfloat16)
            slope = sig + GLU_ALPHA * act * (1.0 - sig)
            d_up = (back * act).astype(jnp.bfloat16)
            d_gate = (back * up_one * slope).astype(jnp.bfloat16)
            hid[rows, cols] = value

            @pl.when(g == 0)
            def _():
                keep = gb if side == 0 else gs
                keep[0, rows, :] = d_gate
                keep[1, rows, :] = d_up
                keep[2, rows, :] = value

    @pl.when(g == 0)
    def _():
        for copy in to_rollout[2:]:
            copy.start()

    @pl.when(g == 1)
    def _():
        for copy in to_rollout:
            copy.wait_recv()

    upper, lower = pl.ds(0, half_rows), pl.ds(half_rows, half_rows)

    def gradient(m, owner):
        left = gdy if m == 2 else gx
        part = lax.dot_general(
            left[owner], gb[m], (((0,), (0,)), ((), ())), preferred_element_type=jnp.float32
        )
        sg[m, owner] = (part * (1.0 / tokens_total)).astype(jnp.bfloat16)

    firsts = {
        m: (
            remote(sg.at[m, dn, upper], r1x.at[m], r1s.at[m, 0], r1r.at[m, 0], x_id),
            remote(sg.at[m, dn, lower], r1y.at[m], r1s.at[m, 1], r1r.at[m, 1], y_id),
        )
        for m in range(3)
    }

    def to_owner(m, i):
        owner, target, land = ((xn, x_id, px), (yn, y_id, py))[i // 2]
        rows = (upper, lower)[i % 2]
        return remote(
            sg.at[m, owner, rows], land.at[m, rows], pps.at[m, i], ppr.at[m, i], target
        )

    lasts = {m: [to_owner(m, i) for i in range(4)] for m in range(3)}

    for m in range(3):
        gradient(m, dn)
        for copy in firsts[m]:
            copy.start()
        gradient(m, xn)
        lasts[m][0].start()
        gradient(m, yn)
        lasts[m][3].start()
    for m in range(3):
        firsts[m][1].wait_recv()
        sg[m, xn, lower, :] = (
            sg[m, xn, lower, :].astype(jnp.float32) + r1y[m].astype(jnp.float32)
        ).astype(jnp.bfloat16)
        lasts[m][1].start()
        firsts[m][0].wait_recv()
        sg[m, yn, upper, :] = (
            sg[m, yn, upper, :].astype(jnp.float32) + r1x[m].astype(jnp.float32)
        ).astype(jnp.bfloat16)
        lasts[m][2].start()

        if m == 0:
            share_rows = row_count // ep_count

            @pl.loop(0, 4)
            def _(c):
                cols = pl.ds(pl.multiple_of(c * dep, dep), dep)
                projected = lax.dot_general(
                    hid[...], wts[2, c], (((1,), (1,)), ((), ())),
                    preferred_element_type=jnp.float32,
                )
                term = (coefs[:, 0:1] * projected).astype(jnp.bfloat16)
                for s in range(steps):
                    spread = lax.dot_general(
                        onehots[s], term[s * CAP : (s + 1) * CAP, :],
                        (((0,), (0,)), ((), ())), preferred_element_type=jnp.float32,
                    ).astype(jnp.bfloat16)
                    for q in range(ep_count):
                        rt[q, s, :, cols] = spread[q * share_rows : (q + 1) * share_rows, :]

            terms = [
                remote(rt.at[peers[k][2]], rr.at[k], es.at[k], er.at[k], peers[k])
                for k in range(ep_count - 1)
            ]
            for copy in terms:
                copy.start()

    for m in range(3):
        gradient(m, f)
    for k in range(ep_count - 1):
        terms[k].wait_recv()
    total = rt[e].astype(jnp.float32)
    for k in range(ep_count - 1):
        total = total + rr[k].astype(jnp.float32)
    lo_out[...] = total.astype(jnp.bfloat16)

    for m in range(3):
        for copy in lasts[m]:
            copy.wait_recv()
        grad_out[m] = (
            sg[m, f].astype(jnp.float32) + px[m].astype(jnp.float32) + py[m].astype(jnp.float32)
        )

    for m in order:
        for copy in (*directs[m], *forwards[m], *shares[m], *firsts[m], *lasts[m]):
            copy.wait_send()
    for copy in terms:
        copy.wait_send()

    @pl.when(g == 0)
    def _():
        for copy in to_rollout:
            copy.wait_send()


def kernel_local(
    batch, expert_ids, route_weights, weights, cotangent, master, moment_one, moment_two
):
    steps, row_count, feat = batch.shape[1:]
    top = expert_ids.shape[3]
    dep, hidden_count = weights.shape[2:]
    half = hidden_count // 2
    slots = steps * CAP
    ep_count = lax.axis_size("ep")
    parts = lax.axis_size("fsdp")
    tokens_total = steps * row_count * parts
    ids = jnp.transpose(expert_ids[0], (2, 0, 1))
    probs = jnp.transpose(route_weights[0], (2, 0, 1))
    vmem = pl.BlockSpec(memory_space=pltpu.VMEM)
    half_b, f32 = jnp.bfloat16, jnp.float32
    dma = pltpu.SemaphoreType.DMA
    layer_out, grad_own = pl.pallas_call(
        functools.partial(layer_kernel, ep_count, tokens_total),
        out_shape=(
            jax.ShapeDtypeStruct((steps, row_count // ep_count, feat), half_b),
            jax.ShapeDtypeStruct((3, dep, half), f32),
        ),
        in_specs=[vmem] * 4 + [pl.BlockSpec(memory_space=pl.ANY)],
        out_specs=(vmem, vmem),
        scratch_shapes=[
            pltpu.VMEM((3, parts, dep, hidden_count), half_b),
            pltpu.VMEM((slots, hidden_count), f32),
            pltpu.VMEM((slots, hidden_count), f32),
            pltpu.VMEM((slots, hidden_count), f32),
            pltpu.VMEM((steps, CAP, row_count), half_b),
            pltpu.VMEM((slots, 128), f32),
            pltpu.VMEM((parts, slots, dep), half_b),
            pltpu.VMEM((parts, slots, dep), half_b),
            pltpu.VMEM((parts, slots, dep), half_b),
            pltpu.VMEM((parts, slots, dep), half_b),
            pltpu.VMEM((slots, hidden_count), half_b),
            pltpu.VMEM((3, slots, half), half_b),
            pltpu.VMEM((3, slots, half), half_b),
            pltpu.VMEM((3, parts, dep, half), half_b),
            pltpu.VMEM((3, dep // 2, half), half_b),
            pltpu.VMEM((3, dep // 2, half), half_b),
            pltpu.VMEM((3, dep, half), half_b),
            pltpu.VMEM((3, dep, half), half_b),
            pltpu.VMEM((ep_count, steps, row_count // ep_count, feat), half_b),
            pltpu.VMEM((ep_count - 1, steps, row_count // ep_count, feat), half_b),
        ]
        + [dma((3,))] * 9
        + [dma((3, 3))] * 2
        + [dma((5,))] * 2
        + [dma((3, 2))] * 2
        + [dma((3, 4))] * 2
        + [dma((ep_count - 1,))] * 2,
        compiler_params=pltpu.CompilerParams(
            collective_id=0, has_side_effects=True, vmem_limit_bytes=62 * 1024 * 1024
        ),
    )(ids, probs, batch[0], cotangent, weights[0])
    master_next, moment_one_next, moment_two_next = adam(
        grad_own[None], master, moment_one, moment_two
    )
    serving = lax.all_gather(master_next.astype(jnp.bfloat16), "group", axis=3, tiled=True)
    return (layer_out[None], master_next, moment_one_next, moment_two_next, serving)


def local(batch, expert_ids, route_weights, weights, cotangent, master, moment_one, moment_two):
    rows_x = batch[0]
    route_ids = expert_ids[0]
    route_probs = route_weights[0]
    step_count, row_count, feat_count = rows_x.shape
    hidden_count = weights.shape[3]
    half_cols = hidden_count // 2
    expert = lax.axis_index("ep")
    core_index = lax.axis_index("group")
    is_learner = core_index == 0
    gathered = lax.all_gather(weights, "fsdp", axis=2, tiled=True)
    w_gate = gathered[0, 0]
    w_up = gathered[0, 1]
    w_down = gathered[0, 2]
    matches = route_ids == expert
    row_coef = jnp.sum(jnp.where(matches, route_probs, jnp.float32(0.0)), axis=2)
    routed = jnp.any(matches, axis=2)
    slot_index = jnp.cumsum(routed.astype(jnp.int32), axis=1) - 1
    slot_iota = lax.broadcasted_iota(jnp.int32, (step_count, CAP, row_count), 1)
    onehot = routed[:, None, :] & (slot_index[:, None, :] == slot_iota)
    picker = onehot.astype(jnp.bfloat16)
    slot_rows = jnp.einsum("scr,srd->scd", picker, rows_x, preferred_element_type=jnp.float32)
    slot_rows = slot_rows.astype(jnp.bfloat16).reshape(step_count * CAP, feat_count)
    slot_coef = jnp.einsum(
        "scr,sr->sc", onehot.astype(jnp.float32), row_coef, precision=lax.Precision.HIGHEST
    )
    gate_pre = jnp.dot(slot_rows, w_gate, preferred_element_type=jnp.float32)
    up_pre = jnp.dot(slot_rows, w_up, preferred_element_type=jnp.float32)
    sig_gate = jax.nn.sigmoid(GLU_ALPHA * gate_pre)
    activated = gate_pre * sig_gate
    hidden = (activated * (up_pre + 1.0)).astype(jnp.bfloat16)
    projected = lax.dot_general(
        hidden, w_down, (((1,), (1,)), ((), ())), preferred_element_type=jnp.float32
    )
    slot_terms = (slot_coef.reshape(-1)[:, None] * projected).astype(jnp.bfloat16)
    slot_terms = slot_terms.reshape(step_count, CAP, feat_count)
    row_terms = jnp.einsum("scr,scd->srd", picker, slot_terms, preferred_element_type=jnp.float32)
    mixed = lax.psum_scatter(row_terms.astype(jnp.bfloat16), "ep", scatter_dimension=1, tiled=True)
    layer_out = mixed[None]
    tokens_total = step_count * row_count * lax.axis_size("fsdp")

    def learner_side(unused):
        dy_slots = jnp.einsum("scr,srd->scd", picker, cotangent, preferred_element_type=jnp.float32)
        dy_scaled = (
            (slot_coef[:, :, None] * dy_slots)
            .astype(jnp.bfloat16)
            .reshape(step_count * CAP, feat_count)
        )
        grad_down = contract_rows(dy_scaled, hidden)
        grad_hidden = jnp.dot(dy_scaled, w_down, preferred_element_type=jnp.float32)
        gate_slope = sig_gate + GLU_ALPHA * gate_pre * sig_gate * (1.0 - sig_gate)
        d_up = (grad_hidden * activated).astype(jnp.bfloat16)
        d_gate = (grad_hidden * (up_pre + 1.0) * gate_slope).astype(jnp.bfloat16)
        grad_gate = contract_rows(slot_rows, d_gate)
        grad_up = contract_rows(slot_rows, d_up)
        return jnp.stack([grad_gate, grad_up, grad_down])[None] / tokens_total

    def rollout_side(unused):
        return jnp.zeros((1, 3, feat_count, hidden_count), jnp.float32)

    grads = lax.cond(is_learner, learner_side, rollout_side, 0)
    crossed = shifted(grads[..., half_cols:].astype(jnp.bfloat16), "group", 1)
    own_terms = jnp.where(is_learner, grads[..., :half_cols].astype(jnp.bfloat16), crossed)
    grad_own = lax.psum_scatter(
        own_terms.astype(jnp.float32).astype(jnp.bfloat16), "fsdp", scatter_dimension=2, tiled=True
    ).astype(jnp.float32)
    moment_one_next = BETA_ONE * moment_one + (1.0 - BETA_ONE) * grad_own
    moment_two_next = BETA_TWO * moment_two + (1.0 - BETA_TWO) * grad_own * grad_own
    master_next = master - LEARN_RATE * (moment_one_next / BIAS_ONE) / (
        jnp.sqrt(moment_two_next / BIAS_TWO) + ADAM_EPS
    )
    serving = lax.all_gather(master_next.astype(jnp.bfloat16), "group", axis=3, tiled=True)
    return (layer_out, master_next, moment_one_next, moment_two_next, serving)


def solution(mesh):
    return jax.shard_map(
        kernel_local if mesh.shape["fsdp"] == 4 else local,
        mesh=mesh,
        in_specs=(
            P("group", None, "fsdp", None),
            P("group", None, "fsdp", None),
            P("group", None, "fsdp", None),
            P("ep", None, "fsdp", None),
            P(None, "fsdp", None),
            P("ep", None, "fsdp", "group"),
            P("ep", None, "fsdp", "group"),
            P("ep", None, "fsdp", "group"),
        ),
        out_specs=(
            P("group", None, ("fsdp", "ep"), None),
            P("ep", None, "fsdp", "group"),
            P("ep", None, "fsdp", "group"),
            P("ep", None, "fsdp", "group"),
            P("ep", None, "fsdp", None),
        ),
        check_vma=False,
    )
```

```python
import functools

import jax
import jax.numpy as jnp
from jax import lax
from jax.experimental import pallas as pl
from jax.experimental.pallas import tpu as pltpu
from jax.sharding import PartitionSpec as P

CAP = 96
MESH = pl.DeviceIdType.MESH
GLU_ALPHA = 1.702
BETA_ONE = 0.9
BETA_TWO = 0.999
LEARN_RATE = 0.01
ADAM_EPS = 1e-08
BIAS_ONE = 1.0 - 0.9**10
BIAS_TWO = 1.0 - 0.999**10


def shifted(value, axis, steps):
    count = lax.axis_size(axis)
    leading, last = (max(0, -steps), min(count, count - steps))
    return lax.ppermute(value, axis, [(source, source + steps) for source in range(leading, last)])


def contract_rows(left, right):
    return lax.dot_general(
        left, right, (((0,), (0,)), ((), ())), preferred_element_type=jnp.float32
    )


def adam(grad_own, master, moment_one, moment_two):
    moment_one_next = BETA_ONE * moment_one + (1.0 - BETA_ONE) * grad_own
    moment_two_next = BETA_TWO * moment_two + (1.0 - BETA_TWO) * grad_own * grad_own
    master_next = master - LEARN_RATE * (moment_one_next / BIAS_ONE) / (
        jnp.sqrt(moment_two_next / BIAS_TWO) + ADAM_EPS
    )
    return master_next, moment_one_next, moment_two_next


def layer_kernel(
    ep_count, tokens_total, ids, probs, x, ct, w, master, moment_one, moment_two,
    lo_out, grad_out, other,
    wts, gate, up, gh, onehots, coefs, xs, dys, gx, gdy, hid, gb, gs, sg,
    r1x, r1y, px, py, rt, rr, sv,
    own_sem, dsx, drx, dsy, dry, fsx, frx, fsy, fry, psend, precv,
    lsend, lrecv, r1s, r1r, pps, ppr, es, er, loads, svs, svr,
):
    g, f, e = lax.axis_index("group"), lax.axis_index("fsdp"), lax.axis_index("ep")
    fx, fy = f % 2, f // 2
    xn, yn, dn, pg = fy * 2 + 1 - fx, (1 - fy) * 2 + fx, 3 - f, 1 - g
    steps, row_count, feat = x.shape
    dep = w.shape[1]
    half_rows, quarter = dep // 2, dep // 4
    hidden_count = w.shape[2]
    half_cols = hidden_count // 2
    slots = steps * CAP
    x_id, y_id, p_id = (g, xn, e), (g, yn, e), (pg, f, e)
    order = (0, 1, 2)
    grad_order = (2, 0, 1)

    barrier = pltpu.get_barrier_semaphore()
    peers = [(g, f, (e + k) % ep_count) for k in range(1, ep_count)]
    greet = [x_id, y_id, p_id] + peers
    for peer in greet:
        pl.semaphore_signal(barrier, inc=1, device_id=peer, device_id_type=MESH)
    pl.semaphore_wait(barrier, len(greet))

    def remote(src, dst, send, recv, target):
        return pltpu.make_async_remote_copy(
            src_ref=src, dst_ref=dst, send_sem=send, recv_sem=recv,
            device_id=target, device_id_type=MESH,
        )

    base = pl.multiple_of(g * half_rows, half_rows)
    mine = pl.ds(base, half_rows)
    first = pl.ds(base, quarter)
    second = pl.ds(pl.multiple_of(base + quarter, quarter), quarter)

    def direct(m):
        return (
            remote(w.at[m, mine], wts.at[m, f, mine], dsx.at[m], drx.at[m], x_id),
            remote(w.at[m, mine], wts.at[m, f, mine], dsy.at[m], dry.at[m], y_id),
        )

    def relays(m):
        return (
            remote(wts.at[m, xn, first], wts.at[m, xn, first], fsy.at[m], fry.at[m], y_id),
            remote(wts.at[m, yn, second], wts.at[m, yn, second], fsx.at[m], frx.at[m], x_id),
        )

    def share(m, place, source):
        block = wts.at[m, source, mine]
        return remote(block, block, psend.at[m, place], precv.at[m, place], p_id)

    directs = {m: direct(m) for m in order}
    forwards = {m: relays(m) for m in order}
    shares = {m: [share(m, i, s) for i, s in enumerate((xn, yn, dn))] for m in order}

    for m in order[:2]:
        for copy in directs[m]:
            copy.start()
    owns = [pltpu.make_async_copy(w.at[m], wts.at[m, f], own_sem.at[m]) for m in range(3)]
    for copy in owns:
        copy.start()

    match = ids[...] == e
    row_coef = jnp.sum(jnp.where(match, probs[...], 0.0), axis=1)
    routed = jnp.max(jnp.where(match, 1.0, 0.0), axis=1)
    before = (
        lax.broadcasted_iota(jnp.int32, (row_count, row_count), 0)
        < lax.broadcasted_iota(jnp.int32, (row_count, row_count), 1)
    )
    rank = jnp.dot(
        routed.astype(jnp.bfloat16),
        jnp.where(before, 1.0, 0.0).astype(jnp.bfloat16),
        preferred_element_type=jnp.float32,
    ).astype(jnp.int32)
    slot_iota = lax.broadcasted_iota(jnp.int32, (CAP, row_count), 0)
    for s in range(steps):
        hit = jnp.where(slot_iota == rank[s : s + 1, :], routed[s : s + 1, :], 0.0)
        onehots[s] = hit.astype(jnp.bfloat16)
        coef = jnp.sum(hit * row_coef[s : s + 1, :], axis=1, keepdims=True)
        coefs[pl.ds(s * CAP, CAP), :] = jnp.broadcast_to(coef, (CAP, 128))

    @pl.loop(0, steps)
    def _(s):
        place = pl.ds(pl.multiple_of(s * CAP, CAP), CAP)
        picker = onehots[s]
        coef = coefs[place, :][:, 0:1]
        for c in range(4):
            cols = pl.ds(c * dep, dep)
            picked = jnp.dot(picker, x[s, :, cols], preferred_element_type=jnp.float32)
            xs[c, place, :] = picked.astype(jnp.bfloat16)
            picked = jnp.dot(picker, ct[s, :, cols], preferred_element_type=jnp.float32)
            dys[c, place, :] = (coef * picked).astype(jnp.bfloat16)

    to_rollout = [
        remote(xs, gx, lsend.at[0], lrecv.at[0], p_id),
        remote(dys, gdy, lsend.at[1], lrecv.at[1], p_id),
    ] + [
        remote(gs.at[i], gb.at[i], lsend.at[2 + i], lrecv.at[2 + i], p_id) for i in range(3)
    ]

    @pl.when(g == 0)
    def _():
        to_rollout[0].start()
        to_rollout[1].start()
        gx[...] = xs[...]
        gdy[...] = dys[...]

    tile = 512

    def accumulate(m, source, start=False):
        total, left = ((gate, xs), (up, xs), (gh, dys))[m]

        @pl.loop(0, hidden_count // tile)
        def _(n):
            cols = pl.ds(pl.multiple_of(n * tile, tile), tile)
            part = jnp.dot(left[source], wts[m, source, :, cols], preferred_element_type=jnp.float32)
            total[:, cols] = part if start else total[:, cols] + part

    for m in order:
        owns[m].wait()
        accumulate(m, f, True)

    def pass_on(m, later=None):
        to_x, to_y = directs[m]
        relay_y, relay_x = forwards[m]
        to_x.wait_recv()
        relay_y.start()
        shares[m][0].start()
        to_y.wait_recv()
        relay_x.start()
        shares[m][1].start()
        if later is not None:
            for copy in directs[later]:
                copy.start()

    def add_direct(m):
        shares[m][0].wait_recv()
        accumulate(m, xn)
        shares[m][1].wait_recv()
        accumulate(m, yn)

    def add_diagonal(m):
        relay_y, relay_x = forwards[m]
        relay_y.wait_recv()
        relay_x.wait_recv()
        shares[m][2].start()
        shares[m][2].wait_recv()
        accumulate(m, dn)

    upper, lower = pl.ds(0, half_rows), pl.ds(half_rows, half_rows)

    def gradient(m, owner):
        left = gdy if m == 2 else gx
        part = lax.dot_general(
            left[owner], gb[m], (((0,), (0,)), ((), ())), preferred_element_type=jnp.float32
        )
        sg[m, owner] = (part * (1.0 / tokens_total)).astype(jnp.bfloat16)

    firsts = {
        m: (
            remote(sg.at[m, dn, upper], r1x.at[m], r1s.at[m, 0], r1r.at[m, 0], x_id),
            remote(sg.at[m, dn, lower], r1y.at[m], r1s.at[m, 1], r1r.at[m, 1], y_id),
        )
        for m in range(3)
    }

    def to_owner(m, i):
        owner, target, land = ((xn, x_id, px), (yn, y_id, py))[i // 2]
        rows = (upper, lower)[i % 2]
        return remote(
            sg.at[m, owner, rows], land.at[m, rows], pps.at[m, i], ppr.at[m, i], target
        )

    lasts = {m: [to_owner(m, i) for i in range(4)] for m in range(3)}

    def open_sum(m):
        gradient(m, dn)
        for copy in firsts[m]:
            copy.start()
        gradient(m, xn)
        lasts[m][0].start()
        gradient(m, yn)
        lasts[m][3].start()

    def relay_sum(m):
        firsts[m][1].wait_recv()
        sg[m, xn, lower, :] = (
            sg[m, xn, lower, :].astype(jnp.float32) + r1y[m].astype(jnp.float32)
        ).astype(jnp.bfloat16)
        lasts[m][1].start()
        firsts[m][0].wait_recv()
        sg[m, yn, upper, :] = (
            sg[m, yn, upper, :].astype(jnp.float32) + r1x[m].astype(jnp.float32)
        ).astype(jnp.bfloat16)
        lasts[m][2].start()

    pass_on(0, 2)
    add_direct(0)
    pass_on(1)
    add_direct(1)
    add_diagonal(0)
    pass_on(2)
    add_diagonal(1)

    block = 16

    @pl.loop(0, slots // block)
    def _(b):
        rows = pl.ds(pl.multiple_of(b * block, block), block)
        for side in range(2):
            cols = pl.ds(side * half_cols, half_cols)
            gate_pre = gate[rows, cols]
            sig = 1.0 / (1.0 + jnp.exp(-GLU_ALPHA * gate_pre))
            value = (gate_pre * sig * (up[rows, cols] + 1.0)).astype(jnp.bfloat16)
            hid[rows, cols] = value

            @pl.when(g == 0)
            def _():
                (gb if side == 0 else gs)[2, rows, :] = value

    @pl.when(g == 0)
    def _():
        to_rollout[4].start()

    @pl.when(g == 1)
    def _():
        for i in (0, 1, 4):
            to_rollout[i].wait_recv()

    open_sum(2)
    add_direct(2)
    add_diagonal(2)

    @pl.when(g == 0)
    def _():
        @pl.loop(0, slots // block)
        def _(b):
            rows = pl.ds(pl.multiple_of(b * block, block), block)
            for side in range(2):
                cols = pl.ds(side * half_cols, half_cols)
                gate_pre, up_one = gate[rows, cols], up[rows, cols] + 1.0
                back = gh[rows, cols]
                sig = 1.0 / (1.0 + jnp.exp(-GLU_ALPHA * gate_pre))
                act = gate_pre * sig
                slope = sig + GLU_ALPHA * act * (1.0 - sig)
                keep = gb if side == 0 else gs
                keep[0, rows, :] = (back * up_one * slope).astype(jnp.bfloat16)
                keep[1, rows, :] = (back * act).astype(jnp.bfloat16)

        to_rollout[2].start()
        to_rollout[3].start()

    def load(i):
        spot = pl.ds((i % 2) * half_cols, half_cols)
        return [
            pltpu.make_async_copy(src.at[grad_order[i]], dst.at[:, spot], loads.at[i, k])
            for k, (src, dst) in enumerate(((master, gate), (moment_one, up), (moment_two, gh)))
        ]

    for i in range(2):
        for copy in load(i):
            copy.start()

    relay_sum(2)

    @pl.when(g == 1)
    def _():
        for i in (2, 3):
            to_rollout[i].wait_recv()

    open_sum(0)
    open_sum(1)

    share_rows = row_count // ep_count

    @pl.loop(0, 4)
    def _(c):
        cols = pl.ds(pl.multiple_of(c * dep, dep), dep)
        projected = lax.dot_general(
            hid[...], wts[2, c], (((1,), (1,)), ((), ())),
            preferred_element_type=jnp.float32,
        )
        term = (coefs[:, 0:1] * projected).astype(jnp.bfloat16)
        for s in range(steps):
            spread = lax.dot_general(
                onehots[s], term[s * CAP : (s + 1) * CAP, :],
                (((0,), (0,)), ((), ())), preferred_element_type=jnp.float32,
            ).astype(jnp.bfloat16)
            for q in range(ep_count):
                rt[q, s, :, cols] = spread[q * share_rows : (q + 1) * share_rows, :]

    terms = [
        remote(rt.at[peers[k][2]], rr.at[k], es.at[k], er.at[k], peers[k])
        for k in range(ep_count - 1)
    ]
    for copy in terms:
        copy.start()

    relay_sum(0)
    relay_sum(1)
    for m in grad_order:
        gradient(m, f)

    servings = [remote(sv.at[m], other.at[m], svs.at[m], svr.at[m], p_id) for m in range(3)]

    def finish(i):
        m = grad_order[i]
        spot = pl.ds((i % 2) * half_cols, half_cols)
        for copy in load(i):
            copy.wait()
        for copy in lasts[m]:
            copy.wait_recv()

        @pl.loop(0, dep // block)
        def _(b):
            rows = pl.ds(pl.multiple_of(b * block, block), block)
            grad = (
                sg[m, f, rows, :].astype(jnp.float32)
                + px[m, rows, :].astype(jnp.float32)
                + py[m, rows, :].astype(jnp.float32)
            )
            grad_out[m, rows, :] = grad
            after = adam(grad, gate[rows, spot], up[rows, spot], gh[rows, spot])[0]
            sv[m, rows, :] = after.astype(jnp.bfloat16)

        servings[m].start()

    finish(0)
    for copy in load(2):
        copy.start()
    finish(1)
    for k in range(ep_count - 1):
        terms[k].wait_recv()
    total = rt[e].astype(jnp.float32)
    for k in range(ep_count - 1):
        total = total + rr[k].astype(jnp.float32)
    lo_out[...] = total.astype(jnp.bfloat16)
    finish(2)
    for copy in servings:
        copy.wait()

    for m in order:
        for copy in (*directs[m], *forwards[m], *shares[m], *firsts[m], *lasts[m]):
            copy.wait_send()
    for copy in terms:
        copy.wait_send()

    @pl.when(g == 0)
    def _():
        for copy in to_rollout:
            copy.wait_send()


def state_kernel(grad, master, moment_one, moment_two, other, master_out, one_out, two_out, serve_out):
    g = lax.axis_index("group")
    half = grad.shape[2]
    after, one, two = adam(grad[...], master[...], moment_one[...], moment_two[...])
    master_out[...] = after
    one_out[...] = one
    two_out[...] = two
    own = after.astype(jnp.bfloat16)

    @pl.when(g == 0)
    def _():
        serve_out[:, :, :half] = own
        serve_out[:, :, half:] = other[...]

    @pl.when(g == 1)
    def _():
        serve_out[:, :, :half] = other[...]
        serve_out[:, :, half:] = own


def kernel_local(
    batch, expert_ids, route_weights, weights, cotangent, master, moment_one, moment_two
):
    steps, row_count, feat = batch.shape[1:]
    top = expert_ids.shape[3]
    dep, hidden_count = weights.shape[2:]
    half = hidden_count // 2
    slots = steps * CAP
    ep_count = lax.axis_size("ep")
    parts = lax.axis_size("fsdp")
    tokens_total = steps * row_count * parts
    ids = jnp.transpose(expert_ids[0], (0, 2, 1))
    probs = jnp.transpose(route_weights[0], (0, 2, 1))
    vmem = pl.BlockSpec(memory_space=pltpu.VMEM)
    half_b, f32 = jnp.bfloat16, jnp.float32
    dma = pltpu.SemaphoreType.DMA
    anywhere = pl.BlockSpec(memory_space=pl.ANY)
    layer_out, grad_own, other = pl.pallas_call(
        functools.partial(layer_kernel, ep_count, tokens_total),
        out_shape=(
            jax.ShapeDtypeStruct((steps, row_count // ep_count, feat), half_b),
            jax.ShapeDtypeStruct((3, dep, half), f32),
            jax.ShapeDtypeStruct((3, dep, half), half_b),
        ),
        in_specs=[vmem] * 4 + [anywhere] * 4,
        out_specs=(vmem, vmem, vmem),
        scratch_shapes=[
            pltpu.VMEM((3, parts, dep, hidden_count), half_b),
            pltpu.VMEM((slots, hidden_count), f32),
            pltpu.VMEM((slots, hidden_count), f32),
            pltpu.VMEM((slots, hidden_count), f32),
            pltpu.VMEM((steps, CAP, row_count), half_b),
            pltpu.VMEM((slots, 128), f32),
            pltpu.VMEM((parts, slots, dep), half_b),
            pltpu.VMEM((parts, slots, dep), half_b),
            pltpu.VMEM((parts, slots, dep), half_b),
            pltpu.VMEM((parts, slots, dep), half_b),
            pltpu.VMEM((slots, hidden_count), half_b),
            pltpu.VMEM((3, slots, half), half_b),
            pltpu.VMEM((3, slots, half), half_b),
            pltpu.VMEM((3, parts, dep, half), half_b),
            pltpu.VMEM((3, dep // 2, half), half_b),
            pltpu.VMEM((3, dep // 2, half), half_b),
            pltpu.VMEM((3, dep, half), half_b),
            pltpu.VMEM((3, dep, half), half_b),
            pltpu.VMEM((ep_count, steps, row_count // ep_count, feat), half_b),
            pltpu.VMEM((ep_count - 1, steps, row_count // ep_count, feat), half_b),
            pltpu.VMEM((3, dep, half), half_b),
        ]
        + [dma((3,))] * 9
        + [dma((3, 3))] * 2
        + [dma((5,))] * 2
        + [dma((3, 2))] * 2
        + [dma((3, 4))] * 2
        + [dma((ep_count - 1,))] * 2
        + [dma((3, 3))]
        + [dma((3,))] * 2,
        compiler_params=pltpu.CompilerParams(
            collective_id=0, has_side_effects=True, vmem_limit_bytes=62 * 1024 * 1024
        ),
    )(ids, probs, batch[0], cotangent, weights[0], master[0], moment_one[0], moment_two[0])
    cut = dep // 4
    narrow = pl.BlockSpec((1, cut, half), lambda m, r: (m, r, 0))
    wide = pl.BlockSpec((1, cut, hidden_count), lambda m, r: (m, r, 0))
    state = jax.ShapeDtypeStruct((3, dep, half), f32)
    master_next, moment_one_next, moment_two_next, serving = pl.pallas_call(
        state_kernel,
        grid=(3, dep // cut),
        out_shape=(state, state, state, jax.ShapeDtypeStruct((3, dep, hidden_count), half_b)),
        in_specs=[narrow] * 5,
        out_specs=(narrow, narrow, narrow, wide),
        compiler_params=pltpu.CompilerParams(vmem_limit_bytes=32 * 1024 * 1024),
    )(grad_own, master[0], moment_one[0], moment_two[0], other)
    return tuple(
        part[None]
        for part in (layer_out, master_next, moment_one_next, moment_two_next, serving)
    )


def local(batch, expert_ids, route_weights, weights, cotangent, master, moment_one, moment_two):
    rows_x = batch[0]
    route_ids = expert_ids[0]
    route_probs = route_weights[0]
    step_count, row_count, feat_count = rows_x.shape
    hidden_count = weights.shape[3]
    half_cols = hidden_count // 2
    expert = lax.axis_index("ep")
    core_index = lax.axis_index("group")
    is_learner = core_index == 0
    gathered = lax.all_gather(weights, "fsdp", axis=2, tiled=True)
    w_gate = gathered[0, 0]
    w_up = gathered[0, 1]
    w_down = gathered[0, 2]
    matches = route_ids == expert
    row_coef = jnp.sum(jnp.where(matches, route_probs, jnp.float32(0.0)), axis=2)
    routed = jnp.any(matches, axis=2)
    slot_index = jnp.cumsum(routed.astype(jnp.int32), axis=1) - 1
    slot_iota = lax.broadcasted_iota(jnp.int32, (step_count, CAP, row_count), 1)
    onehot = routed[:, None, :] & (slot_index[:, None, :] == slot_iota)
    picker = onehot.astype(jnp.bfloat16)
    slot_rows = jnp.einsum("scr,srd->scd", picker, rows_x, preferred_element_type=jnp.float32)
    slot_rows = slot_rows.astype(jnp.bfloat16).reshape(step_count * CAP, feat_count)
    slot_coef = jnp.einsum(
        "scr,sr->sc", onehot.astype(jnp.float32), row_coef, precision=lax.Precision.HIGHEST
    )
    gate_pre = jnp.dot(slot_rows, w_gate, preferred_element_type=jnp.float32)
    up_pre = jnp.dot(slot_rows, w_up, preferred_element_type=jnp.float32)
    sig_gate = jax.nn.sigmoid(GLU_ALPHA * gate_pre)
    activated = gate_pre * sig_gate
    hidden = (activated * (up_pre + 1.0)).astype(jnp.bfloat16)
    projected = lax.dot_general(
        hidden, w_down, (((1,), (1,)), ((), ())), preferred_element_type=jnp.float32
    )
    slot_terms = (slot_coef.reshape(-1)[:, None] * projected).astype(jnp.bfloat16)
    slot_terms = slot_terms.reshape(step_count, CAP, feat_count)
    row_terms = jnp.einsum("scr,scd->srd", picker, slot_terms, preferred_element_type=jnp.float32)
    mixed = lax.psum_scatter(row_terms.astype(jnp.bfloat16), "ep", scatter_dimension=1, tiled=True)
    layer_out = mixed[None]
    tokens_total = step_count * row_count * lax.axis_size("fsdp")

    def learner_side(unused):
        dy_slots = jnp.einsum("scr,srd->scd", picker, cotangent, preferred_element_type=jnp.float32)
        dy_scaled = (
            (slot_coef[:, :, None] * dy_slots)
            .astype(jnp.bfloat16)
            .reshape(step_count * CAP, feat_count)
        )
        grad_down = contract_rows(dy_scaled, hidden)
        grad_hidden = jnp.dot(dy_scaled, w_down, preferred_element_type=jnp.float32)
        gate_slope = sig_gate + GLU_ALPHA * gate_pre * sig_gate * (1.0 - sig_gate)
        d_up = (grad_hidden * activated).astype(jnp.bfloat16)
        d_gate = (grad_hidden * (up_pre + 1.0) * gate_slope).astype(jnp.bfloat16)
        grad_gate = contract_rows(slot_rows, d_gate)
        grad_up = contract_rows(slot_rows, d_up)
        return jnp.stack([grad_gate, grad_up, grad_down])[None] / tokens_total

    def rollout_side(unused):
        return jnp.zeros((1, 3, feat_count, hidden_count), jnp.float32)

    grads = lax.cond(is_learner, learner_side, rollout_side, 0)
    crossed = shifted(grads[..., half_cols:].astype(jnp.bfloat16), "group", 1)
    own_terms = jnp.where(is_learner, grads[..., :half_cols].astype(jnp.bfloat16), crossed)
    grad_own = lax.psum_scatter(
        own_terms.astype(jnp.float32).astype(jnp.bfloat16), "fsdp", scatter_dimension=2, tiled=True
    ).astype(jnp.float32)
    moment_one_next = BETA_ONE * moment_one + (1.0 - BETA_ONE) * grad_own
    moment_two_next = BETA_TWO * moment_two + (1.0 - BETA_TWO) * grad_own * grad_own
    master_next = master - LEARN_RATE * (moment_one_next / BIAS_ONE) / (
        jnp.sqrt(moment_two_next / BIAS_TWO) + ADAM_EPS
    )
    serving = lax.all_gather(master_next.astype(jnp.bfloat16), "group", axis=3, tiled=True)
    return (layer_out, master_next, moment_one_next, moment_two_next, serving)


def solution(mesh):
    return jax.shard_map(
        kernel_local if mesh.shape["fsdp"] == 4 else local,
        mesh=mesh,
        in_specs=(
            P("group", None, "fsdp", None),
            P("group", None, "fsdp", None),
            P("group", None, "fsdp", None),
            P("ep", None, "fsdp", None),
            P(None, "fsdp", None),
            P("ep", None, "fsdp", "group"),
            P("ep", None, "fsdp", "group"),
            P("ep", None, "fsdp", "group"),
        ),
        out_specs=(
            P("group", None, ("fsdp", "ep"), None),
            P("ep", None, "fsdp", "group"),
            P("ep", None, "fsdp", "group"),
            P("ep", None, "fsdp", "group"),
            P("ep", None, "fsdp", None),
        ),
        check_vma=False,
    )
```

```python
import functools

import jax
import jax.numpy as jnp
from jax import lax
from jax.experimental import pallas as pl
from jax.experimental.pallas import tpu as pltpu
from jax.sharding import PartitionSpec as P

CAP = 96
MESH = pl.DeviceIdType.MESH
GLU_ALPHA = 1.702
BETA_ONE = 0.9
BETA_TWO = 0.999
LEARN_RATE = 0.01
ADAM_EPS = 1e-08
BIAS_ONE = 1.0 - 0.9**10
BIAS_TWO = 1.0 - 0.999**10


def shifted(value, axis, steps):
    count = lax.axis_size(axis)
    leading, last = (max(0, -steps), min(count, count - steps))
    return lax.ppermute(value, axis, [(source, source + steps) for source in range(leading, last)])


def contract_rows(left, right):
    return lax.dot_general(
        left, right, (((0,), (0,)), ((), ())), preferred_element_type=jnp.float32
    )


def adam(grad_own, master, moment_one, moment_two):
    moment_one_next = BETA_ONE * moment_one + (1.0 - BETA_ONE) * grad_own
    moment_two_next = BETA_TWO * moment_two + (1.0 - BETA_TWO) * grad_own * grad_own
    master_next = master - LEARN_RATE * (moment_one_next / BIAS_ONE) / (
        jnp.sqrt(moment_two_next / BIAS_TWO) + ADAM_EPS
    )
    return master_next, moment_one_next, moment_two_next


def layer_kernel(
    ep_count, tokens_total, ids, probs, x, ct, w, master, moment_one, moment_two,
    lo_out, grad_out, other,
    wts, gate, up, gh, onehots, coefs, xs, dys, gx, gdy, hid, gb, gs, sg,
    r1x, r1y, px, py, rt, rr, sv,
    own_sem, dsx, drx, dsy, dry, fsx, frx, fsy, fry, psend, precv,
    lsend, lrecv, r1s, r1r, pps, ppr, es, er, loads, svs, svr,
):
    g, f, e = lax.axis_index("group"), lax.axis_index("fsdp"), lax.axis_index("ep")
    fx, fy = f % 2, f // 2
    xn, yn, dn, pg = fy * 2 + 1 - fx, (1 - fy) * 2 + fx, 3 - f, 1 - g
    steps, row_count, feat = x.shape
    dep = w.shape[1]
    half_rows, quarter = dep // 2, dep // 4
    hidden_count = w.shape[2]
    half_cols = hidden_count // 2
    slots = steps * CAP
    x_id, y_id, p_id = (g, xn, e), (g, yn, e), (pg, f, e)
    order = (0, 1, 2)
    grad_order = (2, 0, 1)

    barrier = pltpu.get_barrier_semaphore()
    peers = [(g, f, (e + k) % ep_count) for k in range(1, ep_count)]
    greet = [x_id, y_id, p_id] + peers
    for peer in greet:
        pl.semaphore_signal(barrier, inc=1, device_id=peer, device_id_type=MESH)
    pl.semaphore_wait(barrier, len(greet))

    def remote(src, dst, send, recv, target):
        return pltpu.make_async_remote_copy(
            src_ref=src, dst_ref=dst, send_sem=send, recv_sem=recv,
            device_id=target, device_id_type=MESH,
        )

    base = pl.multiple_of(g * half_rows, half_rows)
    mine = pl.ds(base, half_rows)
    first = pl.ds(base, quarter)
    second = pl.ds(pl.multiple_of(base + quarter, quarter), quarter)

    def direct(m):
        return (
            remote(w.at[m, mine], wts.at[m, f, mine], dsx.at[m], drx.at[m], x_id),
            remote(w.at[m, mine], wts.at[m, f, mine], dsy.at[m], dry.at[m], y_id),
        )

    def relays(m):
        return (
            remote(wts.at[m, xn, first], wts.at[m, xn, first], fsy.at[m], fry.at[m], y_id),
            remote(wts.at[m, yn, second], wts.at[m, yn, second], fsx.at[m], frx.at[m], x_id),
        )

    def share(m, place, source):
        block = wts.at[m, source, mine]
        return remote(block, block, psend.at[m, place], precv.at[m, place], p_id)

    directs = {m: direct(m) for m in order}
    forwards = {m: relays(m) for m in order}
    shares = {m: [share(m, i, s) for i, s in enumerate((xn, yn, dn))] for m in order}

    for m in order[:2]:
        for copy in directs[m]:
            copy.start()
    owns = [pltpu.make_async_copy(w.at[m], wts.at[m, f], own_sem.at[m]) for m in range(3)]
    for copy in owns:
        copy.start()

    match = ids[...] == e
    row_coef = jnp.sum(jnp.where(match, probs[...], 0.0), axis=1)
    routed = jnp.max(jnp.where(match, 1.0, 0.0), axis=1)
    before = (
        lax.broadcasted_iota(jnp.int32, (row_count, row_count), 0)
        < lax.broadcasted_iota(jnp.int32, (row_count, row_count), 1)
    )
    rank = jnp.dot(
        routed.astype(jnp.bfloat16),
        jnp.where(before, 1.0, 0.0).astype(jnp.bfloat16),
        preferred_element_type=jnp.float32,
    ).astype(jnp.int32)
    slot_iota = lax.broadcasted_iota(jnp.int32, (CAP, row_count), 0)
    for s in range(steps):
        hit = jnp.where(slot_iota == rank[s : s + 1, :], routed[s : s + 1, :], 0.0)
        onehots[s] = hit.astype(jnp.bfloat16)
        coef = jnp.sum(hit * row_coef[s : s + 1, :], axis=1, keepdims=True)
        coefs[pl.ds(s * CAP, CAP), :] = jnp.broadcast_to(coef, (CAP, 128))

    @pl.loop(0, steps)
    def _(s):
        place = pl.ds(pl.multiple_of(s * CAP, CAP), CAP)
        picker = onehots[s]
        coef = coefs[place, :][:, 0:1]
        for c in range(4):
            cols = pl.ds(c * dep, dep)
            picked = jnp.dot(picker, x[s, :, cols], preferred_element_type=jnp.float32)
            xs[c, place, :] = picked.astype(jnp.bfloat16)
            picked = jnp.dot(picker, ct[s, :, cols], preferred_element_type=jnp.float32)
            dys[c, place, :] = (coef * picked).astype(jnp.bfloat16)

    to_rollout = [
        remote(xs, gx, lsend.at[0], lrecv.at[0], p_id),
        remote(dys, gdy, lsend.at[1], lrecv.at[1], p_id),
    ] + [
        remote(gs.at[i], gb.at[i], lsend.at[2 + i], lrecv.at[2 + i], p_id) for i in range(3)
    ]

    @pl.when(g == 0)
    def _():
        to_rollout[0].start()
        to_rollout[1].start()
        gx[...] = xs[...]
        gdy[...] = dys[...]

    tile = 512

    def accumulate(m, source, start=False):
        total, left = ((gate, xs), (up, xs), (gh, dys))[m]

        @pl.loop(0, hidden_count // tile)
        def _(n):
            cols = pl.ds(pl.multiple_of(n * tile, tile), tile)
            part = jnp.dot(left[source], wts[m, source, :, cols], preferred_element_type=jnp.float32)
            total[:, cols] = part if start else total[:, cols] + part

    for m in order:
        owns[m].wait()
        accumulate(m, f, True)

    def pass_on(m, later=None):
        to_x, to_y = directs[m]
        relay_y, relay_x = forwards[m]
        to_x.wait_recv()
        relay_y.start()
        shares[m][0].start()
        to_y.wait_recv()
        relay_x.start()
        shares[m][1].start()
        if later is not None:
            for copy in directs[later]:
                copy.start()

    def add_direct(m):
        shares[m][0].wait_recv()
        accumulate(m, xn)
        shares[m][1].wait_recv()
        accumulate(m, yn)

    def add_diagonal(m):
        relay_y, relay_x = forwards[m]
        relay_y.wait_recv()
        relay_x.wait_recv()
        shares[m][2].start()
        shares[m][2].wait_recv()
        accumulate(m, dn)

    upper, lower = pl.ds(0, half_rows), pl.ds(half_rows, half_rows)

    def gradient(m, owner):
        left = gdy if m == 2 else gx
        part = lax.dot_general(
            left[owner], gb[m], (((0,), (0,)), ((), ())), preferred_element_type=jnp.float32
        )
        sg[m, owner] = (part * (1.0 / tokens_total)).astype(jnp.bfloat16)

    firsts = {
        m: (
            remote(sg.at[m, dn, upper], r1x.at[m], r1s.at[m, 0], r1r.at[m, 0], x_id),
            remote(sg.at[m, dn, lower], r1y.at[m], r1s.at[m, 1], r1r.at[m, 1], y_id),
        )
        for m in range(3)
    }

    def to_owner(m, i):
        owner, target, land = ((xn, x_id, px), (yn, y_id, py))[i // 2]
        rows = (upper, lower)[i % 2]
        return remote(
            sg.at[m, owner, rows], land.at[m, rows], pps.at[m, i], ppr.at[m, i], target
        )

    lasts = {m: [to_owner(m, i) for i in range(4)] for m in range(3)}

    def open_sum(*matrices):
        for m in matrices:
            gradient(m, dn)
            for copy in firsts[m]:
                copy.start()
        for m in matrices:
            gradient(m, xn)
            lasts[m][0].start()
            gradient(m, yn)
            lasts[m][3].start()

    def relay_sum(m):
        firsts[m][1].wait_recv()
        sg[m, xn, lower, :] = (
            sg[m, xn, lower, :].astype(jnp.float32) + r1y[m].astype(jnp.float32)
        ).astype(jnp.bfloat16)
        lasts[m][1].start()
        firsts[m][0].wait_recv()
        sg[m, yn, upper, :] = (
            sg[m, yn, upper, :].astype(jnp.float32) + r1x[m].astype(jnp.float32)
        ).astype(jnp.bfloat16)
        lasts[m][2].start()

    pass_on(0, 2)
    add_direct(0)
    pass_on(1)
    add_direct(1)
    add_diagonal(0)
    pass_on(2)
    add_diagonal(1)

    block = 16

    @pl.loop(0, slots // block)
    def _(b):
        rows = pl.ds(pl.multiple_of(b * block, block), block)
        for side in range(2):
            cols = pl.ds(side * half_cols, half_cols)
            gate_pre = gate[rows, cols]
            sig = 1.0 / (1.0 + jnp.exp(-GLU_ALPHA * gate_pre))
            value = (gate_pre * sig * (up[rows, cols] + 1.0)).astype(jnp.bfloat16)
            hid[rows, cols] = value

            @pl.when(g == 0)
            def _():
                (gb if side == 0 else gs)[2, rows, :] = value

    @pl.when(g == 0)
    def _():
        to_rollout[4].start()

    @pl.when(g == 1)
    def _():
        for i in (0, 1, 4):
            to_rollout[i].wait_recv()

    open_sum(2)
    add_direct(2)
    add_diagonal(2)

    @pl.when(g == 0)
    def _():
        @pl.loop(0, slots // block)
        def _(b):
            rows = pl.ds(pl.multiple_of(b * block, block), block)
            for side in range(2):
                cols = pl.ds(side * half_cols, half_cols)
                gate_pre, up_one = gate[rows, cols], up[rows, cols] + 1.0
                back = gh[rows, cols]
                sig = 1.0 / (1.0 + jnp.exp(-GLU_ALPHA * gate_pre))
                act = gate_pre * sig
                slope = sig + GLU_ALPHA * act * (1.0 - sig)
                keep = gb if side == 0 else gs
                keep[0, rows, :] = (back * up_one * slope).astype(jnp.bfloat16)
                keep[1, rows, :] = (back * act).astype(jnp.bfloat16)

        to_rollout[2].start()
        to_rollout[3].start()

    def load(i):
        spot = pl.ds((i % 2) * half_cols, half_cols)
        return [
            pltpu.make_async_copy(src.at[grad_order[i]], dst.at[:, spot], loads.at[i, k])
            for k, (src, dst) in enumerate(((master, gate), (moment_one, up), (moment_two, gh)))
        ]

    for i in range(2):
        for copy in load(i):
            copy.start()

    relay_sum(2)

    @pl.when(g == 1)
    def _():
        for i in (2, 3):
            to_rollout[i].wait_recv()

    open_sum(0, 1)

    share_rows = row_count // ep_count

    @pl.loop(0, 4)
    def _(c):
        cols = pl.ds(pl.multiple_of(c * dep, dep), dep)
        projected = lax.dot_general(
            hid[...], wts[2, c], (((1,), (1,)), ((), ())),
            preferred_element_type=jnp.float32,
        )
        term = (coefs[:, 0:1] * projected).astype(jnp.bfloat16)
        for s in range(steps):
            spread = lax.dot_general(
                onehots[s], term[s * CAP : (s + 1) * CAP, :],
                (((0,), (0,)), ((), ())), preferred_element_type=jnp.float32,
            ).astype(jnp.bfloat16)
            for q in range(ep_count):
                rt[q, s, :, cols] = spread[q * share_rows : (q + 1) * share_rows, :]

    terms = [
        remote(rt.at[peers[k][2]], rr.at[k], es.at[k], er.at[k], peers[k])
        for k in range(ep_count - 1)
    ]
    for copy in terms:
        copy.start()

    relay_sum(0)
    relay_sum(1)
    for m in grad_order:
        gradient(m, f)

    servings = [remote(sv.at[m], other.at[m], svs.at[m], svr.at[m], p_id) for m in range(3)]

    def finish(i):
        m = grad_order[i]
        spot = pl.ds((i % 2) * half_cols, half_cols)
        for copy in load(i):
            copy.wait()
        for copy in lasts[m]:
            copy.wait_recv()

        @pl.loop(0, dep // block)
        def _(b):
            rows = pl.ds(pl.multiple_of(b * block, block), block)
            grad = (
                sg[m, f, rows, :].astype(jnp.float32)
                + px[m, rows, :].astype(jnp.float32)
                + py[m, rows, :].astype(jnp.float32)
            )
            grad_out[m, rows, :] = grad
            after = adam(grad, gate[rows, spot], up[rows, spot], gh[rows, spot])[0]
            sv[m, rows, :] = after.astype(jnp.bfloat16)

        servings[m].start()

    finish(0)
    for copy in load(2):
        copy.start()
    finish(1)
    for k in range(ep_count - 1):
        terms[k].wait_recv()
    total = rt[e].astype(jnp.float32)
    for k in range(ep_count - 1):
        total = total + rr[k].astype(jnp.float32)
    lo_out[...] = total.astype(jnp.bfloat16)
    finish(2)
    for copy in servings:
        copy.wait()

    for m in order:
        for copy in (*directs[m], *forwards[m], *shares[m], *firsts[m], *lasts[m]):
            copy.wait_send()
    for copy in terms:
        copy.wait_send()

    @pl.when(g == 0)
    def _():
        for copy in to_rollout:
            copy.wait_send()


def state_kernel(grad, master, moment_one, moment_two, other, master_out, one_out, two_out, serve_out):
    g = lax.axis_index("group")
    half = grad.shape[2]
    block = 16

    def write(own_cols, other_cols):
        @pl.loop(0, grad.shape[1] // block)
        def _(b):
            rows = pl.ds(pl.multiple_of(b * block, block), block)
            after, one, two = adam(
                grad[0, rows, :], master[0, rows, :], moment_one[0, rows, :], moment_two[0, rows, :]
            )
            master_out[0, rows, :] = after
            one_out[0, rows, :] = one
            two_out[0, rows, :] = two
            serve_out[0, rows, own_cols] = after.astype(jnp.bfloat16)
            serve_out[0, rows, other_cols] = other[0, rows, :]

    low, high = pl.ds(0, half), pl.ds(half, half)

    @pl.when(g == 0)
    def _():
        write(low, high)

    @pl.when(g == 1)
    def _():
        write(high, low)


def kernel_local(
    batch, expert_ids, route_weights, weights, cotangent, master, moment_one, moment_two
):
    steps, row_count, feat = batch.shape[1:]
    top = expert_ids.shape[3]
    dep, hidden_count = weights.shape[2:]
    half = hidden_count // 2
    slots = steps * CAP
    ep_count = lax.axis_size("ep")
    parts = lax.axis_size("fsdp")
    tokens_total = steps * row_count * parts
    ids = jnp.transpose(expert_ids[0], (0, 2, 1))
    probs = jnp.transpose(route_weights[0], (0, 2, 1))
    vmem = pl.BlockSpec(memory_space=pltpu.VMEM)
    half_b, f32 = jnp.bfloat16, jnp.float32
    dma = pltpu.SemaphoreType.DMA
    anywhere = pl.BlockSpec(memory_space=pl.ANY)
    layer_out, grad_own, other = pl.pallas_call(
        functools.partial(layer_kernel, ep_count, tokens_total),
        out_shape=(
            jax.ShapeDtypeStruct((steps, row_count // ep_count, feat), half_b),
            jax.ShapeDtypeStruct((3, dep, half), f32),
            jax.ShapeDtypeStruct((3, dep, half), half_b),
        ),
        in_specs=[vmem] * 4 + [anywhere] * 4,
        out_specs=(vmem, vmem, vmem),
        scratch_shapes=[
            pltpu.VMEM((3, parts, dep, hidden_count), half_b),
            pltpu.VMEM((slots, hidden_count), f32),
            pltpu.VMEM((slots, hidden_count), f32),
            pltpu.VMEM((slots, hidden_count), f32),
            pltpu.VMEM((steps, CAP, row_count), half_b),
            pltpu.VMEM((slots, 128), f32),
            pltpu.VMEM((parts, slots, dep), half_b),
            pltpu.VMEM((parts, slots, dep), half_b),
            pltpu.VMEM((parts, slots, dep), half_b),
            pltpu.VMEM((parts, slots, dep), half_b),
            pltpu.VMEM((slots, hidden_count), half_b),
            pltpu.VMEM((3, slots, half), half_b),
            pltpu.VMEM((3, slots, half), half_b),
            pltpu.VMEM((3, parts, dep, half), half_b),
            pltpu.VMEM((3, dep // 2, half), half_b),
            pltpu.VMEM((3, dep // 2, half), half_b),
            pltpu.VMEM((3, dep, half), half_b),
            pltpu.VMEM((3, dep, half), half_b),
            pltpu.VMEM((ep_count, steps, row_count // ep_count, feat), half_b),
            pltpu.VMEM((ep_count - 1, steps, row_count // ep_count, feat), half_b),
            pltpu.VMEM((3, dep, half), half_b),
        ]
        + [dma((3,))] * 9
        + [dma((3, 3))] * 2
        + [dma((5,))] * 2
        + [dma((3, 2))] * 2
        + [dma((3, 4))] * 2
        + [dma((ep_count - 1,))] * 2
        + [dma((3, 3))]
        + [dma((3,))] * 2,
        compiler_params=pltpu.CompilerParams(
            collective_id=0, has_side_effects=True, vmem_limit_bytes=62 * 1024 * 1024
        ),
    )(ids, probs, batch[0], cotangent, weights[0], master[0], moment_one[0], moment_two[0])
    cut = dep // 2
    narrow = pl.BlockSpec((1, cut, half), lambda m, r: (m, r, 0))
    wide = pl.BlockSpec((1, cut, hidden_count), lambda m, r: (m, r, 0))
    state = jax.ShapeDtypeStruct((3, dep, half), f32)
    master_next, moment_one_next, moment_two_next, serving = pl.pallas_call(
        state_kernel,
        grid=(3, dep // cut),
        out_shape=(state, state, state, jax.ShapeDtypeStruct((3, dep, hidden_count), half_b)),
        in_specs=[narrow] * 5,
        out_specs=(narrow, narrow, narrow, wide),
        compiler_params=pltpu.CompilerParams(vmem_limit_bytes=60 * 1024 * 1024),
    )(grad_own, master[0], moment_one[0], moment_two[0], other)
    return tuple(
        part[None]
        for part in (layer_out, master_next, moment_one_next, moment_two_next, serving)
    )


def local(batch, expert_ids, route_weights, weights, cotangent, master, moment_one, moment_two):
    rows_x = batch[0]
    route_ids = expert_ids[0]
    route_probs = route_weights[0]
    step_count, row_count, feat_count = rows_x.shape
    hidden_count = weights.shape[3]
    half_cols = hidden_count // 2
    expert = lax.axis_index("ep")
    core_index = lax.axis_index("group")
    is_learner = core_index == 0
    gathered = lax.all_gather(weights, "fsdp", axis=2, tiled=True)
    w_gate = gathered[0, 0]
    w_up = gathered[0, 1]
    w_down = gathered[0, 2]
    matches = route_ids == expert
    row_coef = jnp.sum(jnp.where(matches, route_probs, jnp.float32(0.0)), axis=2)
    routed = jnp.any(matches, axis=2)
    slot_index = jnp.cumsum(routed.astype(jnp.int32), axis=1) - 1
    slot_iota = lax.broadcasted_iota(jnp.int32, (step_count, CAP, row_count), 1)
    onehot = routed[:, None, :] & (slot_index[:, None, :] == slot_iota)
    picker = onehot.astype(jnp.bfloat16)
    slot_rows = jnp.einsum("scr,srd->scd", picker, rows_x, preferred_element_type=jnp.float32)
    slot_rows = slot_rows.astype(jnp.bfloat16).reshape(step_count * CAP, feat_count)
    slot_coef = jnp.einsum(
        "scr,sr->sc", onehot.astype(jnp.float32), row_coef, precision=lax.Precision.HIGHEST
    )
    gate_pre = jnp.dot(slot_rows, w_gate, preferred_element_type=jnp.float32)
    up_pre = jnp.dot(slot_rows, w_up, preferred_element_type=jnp.float32)
    sig_gate = jax.nn.sigmoid(GLU_ALPHA * gate_pre)
    activated = gate_pre * sig_gate
    hidden = (activated * (up_pre + 1.0)).astype(jnp.bfloat16)
    projected = lax.dot_general(
        hidden, w_down, (((1,), (1,)), ((), ())), preferred_element_type=jnp.float32
    )
    slot_terms = (slot_coef.reshape(-1)[:, None] * projected).astype(jnp.bfloat16)
    slot_terms = slot_terms.reshape(step_count, CAP, feat_count)
    row_terms = jnp.einsum("scr,scd->srd", picker, slot_terms, preferred_element_type=jnp.float32)
    mixed = lax.psum_scatter(row_terms.astype(jnp.bfloat16), "ep", scatter_dimension=1, tiled=True)
    layer_out = mixed[None]
    tokens_total = step_count * row_count * lax.axis_size("fsdp")

    def learner_side(unused):
        dy_slots = jnp.einsum("scr,srd->scd", picker, cotangent, preferred_element_type=jnp.float32)
        dy_scaled = (
            (slot_coef[:, :, None] * dy_slots)
            .astype(jnp.bfloat16)
            .reshape(step_count * CAP, feat_count)
        )
        grad_down = contract_rows(dy_scaled, hidden)
        grad_hidden = jnp.dot(dy_scaled, w_down, preferred_element_type=jnp.float32)
        gate_slope = sig_gate + GLU_ALPHA * gate_pre * sig_gate * (1.0 - sig_gate)
        d_up = (grad_hidden * activated).astype(jnp.bfloat16)
        d_gate = (grad_hidden * (up_pre + 1.0) * gate_slope).astype(jnp.bfloat16)
        grad_gate = contract_rows(slot_rows, d_gate)
        grad_up = contract_rows(slot_rows, d_up)
        return jnp.stack([grad_gate, grad_up, grad_down])[None] / tokens_total

    def rollout_side(unused):
        return jnp.zeros((1, 3, feat_count, hidden_count), jnp.float32)

    grads = lax.cond(is_learner, learner_side, rollout_side, 0)
    crossed = shifted(grads[..., half_cols:].astype(jnp.bfloat16), "group", 1)
    own_terms = jnp.where(is_learner, grads[..., :half_cols].astype(jnp.bfloat16), crossed)
    grad_own = lax.psum_scatter(
        own_terms.astype(jnp.float32).astype(jnp.bfloat16), "fsdp", scatter_dimension=2, tiled=True
    ).astype(jnp.float32)
    moment_one_next = BETA_ONE * moment_one + (1.0 - BETA_ONE) * grad_own
    moment_two_next = BETA_TWO * moment_two + (1.0 - BETA_TWO) * grad_own * grad_own
    master_next = master - LEARN_RATE * (moment_one_next / BIAS_ONE) / (
        jnp.sqrt(moment_two_next / BIAS_TWO) + ADAM_EPS
    )
    serving = lax.all_gather(master_next.astype(jnp.bfloat16), "group", axis=3, tiled=True)
    return (layer_out, master_next, moment_one_next, moment_two_next, serving)


def solution(mesh):
    return jax.shard_map(
        kernel_local if mesh.shape["fsdp"] == 4 else local,
        mesh=mesh,
        in_specs=(
            P("group", None, "fsdp", None),
            P("group", None, "fsdp", None),
            P("group", None, "fsdp", None),
            P("ep", None, "fsdp", None),
            P(None, "fsdp", None),
            P("ep", None, "fsdp", "group"),
            P("ep", None, "fsdp", "group"),
            P("ep", None, "fsdp", "group"),
        ),
        out_specs=(
            P("group", None, ("fsdp", "ep"), None),
            P("ep", None, "fsdp", "group"),
            P("ep", None, "fsdp", "group"),
            P("ep", None, "fsdp", "group"),
            P("ep", None, "fsdp", None),
        ),
        check_vma=False,
    )
```
